32 devices in a mesh: dp: 8 (over y, x, core), blk: 4 (over z).
Axes of the slice: x: 2, y: 2, z: 4, core: 2. Of those that a mesh axis runs over, the one named last changes fastest.
Arguments:
- captions: bfloat16 [512, 1152], P('dp'), may hold values from -6 to 6
- w_in: bfloat16 [1152, 4096], P(None, 'blk'), may hold values from -0.1875 to 0.1875
- w_out: bfloat16 [4096, 1152], P('blk'), may hold values from -0.09375 to 0.09375
- images: bfloat16 [128, 1152], P('blk'), may hold values from -6 to 6
- pairs: int32 [512], P('dp'), may hold values from 0 to 127
Outputs:
- grad_w_in: float32 [1152, 4096], P('dp', 'blk')
- grad_w_out_t: float32 [1152, 4096], P('dp', 'blk')
The draws below stay inside these ranges and needn't reach their ends.
All inputs are finite; a program needn't handle non-finite values.
Results may differ from the reference program's by a relative error of at most 0.005.
Values may be sent and summed in bfloat16 or wider, within the bound.
A program may use at most 64 MiB of HBM per device.

```python
import jax
import jax.numpy as jnp
from jax import lax

D = 1152
FF = 4096
CAPS = 512
IMGS = 128


def set_ends(entries, stream_key, low, high):
    longest = entries.shape.index(max(entries.shape))
    spots = []
    for shift in (0, 1):
        where = [jax.random.randint(jax.random.fold_in(stream_key, axis), (), 0, length) for axis, length in enumerate(entries.shape)]
        where[longest] = (where[longest] + shift) % entries.shape[longest]
        spots.append(tuple(where))
    return entries.at[spots[0]].set(low).at[spots[1]].set(high)


def block_levels(rng, extent, cuts, smallest, high):
    loudness, own = 1.0, jax.random.fold_in(rng, 6)
    for dim, parts in cuts:
        draws = jnp.exp(jax.random.uniform(jax.random.fold_in(own, dim), (parts,), jnp.float32, smallest / len(cuts), high / len(cuts)))
        loudness = loudness * jnp.repeat(draws, extent[dim] // parts).reshape([-1 if axis == dim else 1 for axis in range(len(extent))])
    return loudness


def normal_values(stream_key, shape, scale, limit, pieces=(), held_as=jnp.bfloat16):
    drawn = jax.random.normal(stream_key, shape, jnp.float32) * scale
    if len(pieces) > 0:
        drawn = block_levels(stream_key, shape, pieces, -0.22, 0.18) * drawn
    return jnp.clip(drawn, min=-limit, max=limit).astype(held_as)


def setup_inputs(seed: int = 0) -> dict:
    arg_keys = jax.random.split(jax.random.key(seed), 6)
    captions = normal_values(arg_keys[0], (CAPS, D), 1.0, 6.0, ((0, 8),))
    w_in = normal_values(arg_keys[1], (D, FF), D ** -0.5, 0.1875, ((1, 4),))
    w_out = normal_values(arg_keys[2], (FF, D), FF ** -0.5, 0.09375, ((0, 4),))
    images = normal_values(arg_keys[3], (IMGS, D), 1.0, 6.0, ((0, 4),))
    pairs = set_ends(jax.random.randint(arg_keys[4], (CAPS,), 0, IMGS), jax.random.fold_in(arg_keys[4], 1), 0, IMGS - 1).astype(jnp.int32)
    return {"captions": captions, "w_in": w_in, "w_out": w_out, "images": images, "pairs": pairs}


SCORE_SCALE = 10.0
SCORE_BIAS_TERM = -5.0
EPSILON = 1e-06

def activate(values):
    return jax.nn.gelu(values, approximate=True)

def reference(captions, w_in, w_out, images, pairs):
    pre_act = jnp.dot(captions, w_in, preferred_element_type=jnp.float32)
    hidden = activate(pre_act).astype(jnp.bfloat16)
    embedding = jnp.dot(hidden, w_out, preferred_element_type=jnp.float32)
    inv_norm = lax.rsqrt(lax.optimization_barrier(jnp.sum(embedding * embedding, axis=1, keepdims=True)) + EPSILON)
    unit_dir = embedding * inv_norm
    direction_halfway = unit_dir.astype(jnp.bfloat16)
    image_vals = images.astype(jnp.float32)
    image_direction = (image_vals * lax.rsqrt(lax.optimization_barrier(jnp.sum(image_vals * image_vals, axis=1, keepdims=True)) + EPSILON)).astype(jnp.bfloat16)
    pair_scores = SCORE_SCALE * jnp.dot(direction_halfway, image_direction.T, preferred_element_type=jnp.float32) + SCORE_BIAS_TERM
    columns = jnp.arange(IMGS, dtype=jnp.int32)
    labels = (pairs[:, None] == columns[None, :]).astype(jnp.float32)
    label_error = (jax.nn.sigmoid(pair_scores) - labels).astype(jnp.bfloat16)
    direction_gradient = SCORE_SCALE * jnp.dot(label_error, image_direction, preferred_element_type=jnp.float32)
    embed_grad = (direction_gradient - unit_dir * lax.optimization_barrier(jnp.sum(unit_dir * direction_gradient, axis=1, keepdims=True))) * inv_norm
    embed_half = embed_grad.astype(jnp.bfloat16)
    hidden_grad = jnp.dot(embed_half, w_out.T, preferred_element_type=jnp.float32)
    _, pullback = jax.vjp(activate, pre_act)
    preact_grad = pullback(hidden_grad)[0].astype(jnp.bfloat16)
    grad_w_in = jnp.dot(captions.T, preact_grad, preferred_element_type=jnp.float32)
    grad_w_out_t = jnp.dot(embed_half.T, hidden, preferred_element_type=jnp.float32)
    return (grad_w_in, grad_w_out_t)
```

```python
import functools

import jax
import jax.numpy as jnp
from jax import lax
from jax.experimental import pallas as pl
from jax.experimental.pallas import tpu as pltpu
from jax.sharding import PartitionSpec as P

SCORE_SCALE = 10.0
SCORE_BIAS_TERM = -5.0
EPSILON = 1e-06


def from_behind(block, axis, distance):
    devices = range(lax.axis_size(axis))
    route = [((i - distance) % len(devices), i) for i in devices]
    return lax.ppermute(block, axis, route)


def activate(values):
    return jax.nn.gelu(values, approximate=True)


def tile_grad(direction_halfway, image_direction, first_image, row_pairs):
    pair_scores = (
        SCORE_SCALE
        * lax.dot_general(
            direction_halfway,
            image_direction,
            (((1,), (1,)), ((), ())),
            preferred_element_type=jnp.float32,
        )
        + SCORE_BIAS_TERM
    )
    columns = first_image + lax.broadcasted_iota(jnp.int32, pair_scores.shape, 1)
    labels = (row_pairs[:, None] == columns).astype(jnp.float32)
    label_error = (jax.nn.sigmoid(pair_scores) - labels).astype(jnp.bfloat16)
    return SCORE_SCALE * jnp.dot(label_error, image_direction, preferred_element_type=jnp.float32)


def staged_body(captions, w_in, w_out, images, pairs):
    cycle_size = lax.axis_size("blk")
    cycle_pos = lax.axis_index("blk")
    own_rows = captions.shape[0] // cycle_size
    block_len = images.shape[0]
    width = captions.shape[1]
    pre_act = jnp.dot(captions, w_in, preferred_element_type=jnp.float32)
    hidden = activate(pre_act).astype(jnp.bfloat16)
    rows_hidden = hidden
    embedding = lax.psum_scatter(
        jnp.dot(rows_hidden, w_out, preferred_element_type=jnp.float32),
        "blk",
        scatter_dimension=0,
        tiled=True,
    )
    inv_norm = lax.rsqrt(jnp.sum(embedding * embedding, axis=1, keepdims=True) + EPSILON)
    unit_dir = embedding * inv_norm
    direction_halfway = unit_dir.astype(jnp.bfloat16)
    image_vals = images.astype(jnp.float32)
    image_direction = (
        image_vals * lax.rsqrt(jnp.sum(image_vals * image_vals, axis=1, keepdims=True) + EPSILON)
    ).astype(jnp.bfloat16)
    row_pairs = lax.dynamic_slice_in_dim(pairs, cycle_pos * own_rows, own_rows, 0)

    def visit(step, carry):
        running, block = carry
        source = (cycle_pos - step) % cycle_size
        running = running + tile_grad(direction_halfway, block, source * block_len, row_pairs)
        block = from_behind(block, "blk", 1)
        return (running, block)

    start_sum = jnp.zeros((own_rows, width), jnp.float32)
    running, block = lax.fori_loop(0, cycle_size - 1, visit, (start_sum, image_direction))
    source = (cycle_pos - (cycle_size - 1)) % cycle_size
    direction_gradient = running + tile_grad(
        direction_halfway, block, source * block_len, row_pairs
    )
    embed_grad = (
        direction_gradient
        - unit_dir * jnp.sum(unit_dir * direction_gradient, axis=1, keepdims=True)
    ) * inv_norm
    embed_half = embed_grad.astype(jnp.bfloat16)
    piece = lax.all_gather(embed_half, "blk", axis=0, tiled=True)
    rows_hidden = hidden
    hidden_grad = lax.dot_general(
        piece, w_out, (((1,), (1,)), ((), ())), preferred_element_type=jnp.float32
    )
    _, pullback = jax.vjp(activate, pre_act)
    preact_grad = pullback(hidden_grad)[0].astype(jnp.bfloat16)
    grad_in = lax.dot_general(
        captions, preact_grad, (((0,), (0,)), ((), ())), preferred_element_type=jnp.float32
    )
    grad_out = lax.dot_general(
        piece, rows_hidden, (((0,), (0,)), ((), ())), preferred_element_type=jnp.float32
    )
    grad_in, grad_out = (grad_in, grad_out)
    grad_w_in, grad_w_out_t = (
        lax.psum_scatter(grad_in, "dp", scatter_dimension=0, tiled=True),
        lax.psum_scatter(grad_out, "dp", scatter_dimension=0, tiled=True),
    )
    return (grad_w_in, grad_w_out_t)


MESH = pl.DeviceIdType.MESH
CHUNK = 256
VMEM_BYTES = 60 * 2**20
GELU_SCALE = 0.7978845608028654
GELU_CUBE = 0.044715
NT = (((1,), (1,)), ((), ()))


def gelu_and_slope(v):
    square = v * v
    t = jnp.tanh(GELU_SCALE * (v + GELU_CUBE * (square * v)))
    half = 0.5 * (1.0 + t)
    slope = half + (0.5 * GELU_SCALE) * v * (1.0 - t * t) * (1.0 + (3.0 * GELU_CUBE) * square)
    return v * half, slope


def head_kernel(
    nd, nb,
    caps_hbm, win_hbm, wout_hbm, img_hbm, pairs, gin_hbm, gout_hbm,
    win, wout, img, imgu, caps, emb, part, rs_send, rs_recv, hidden, slope, pgrad,
    pick, caps_t, emb_t, gin, gout,
    load_sem, store_sem,
    cap_send, cap_recv, cap_fsend, cap_frecv,
    img_send, img_recv, img_fsend, img_frecv,
    rs_ssem, rs_rsem,
    ez_send, ez_recv, ex_send, ex_recv, ef_send, ef_recv,
):
    d = lax.axis_index("dp")
    b = lax.axis_index("blk")
    core = d % 2
    chip = d // 2
    nc = nd // 2
    sibling = chip * 2 + (1 - core)
    rows, width = caps_hbm.shape
    ff = win_hbm.shape[1]
    per = img_hbm.shape[0]
    half = per // 2
    piece = rows // nb
    outs = gin.shape[0]

    def z_at(k):
        return (b + k) % nb

    def z_from(k):
        return (b + nb - k) % nb

    def chip_at(k):
        return (chip + k) % nc

    def chip_from(k):
        return (chip + nc - k) % nc

    def dev_rows(dev):
        return pl.ds(pl.multiple_of(dev * rows, rows), rows)

    def chip_rows(c):
        return pl.ds(pl.multiple_of(c * (2 * rows), 2 * rows), 2 * rows)

    def piece_rows(dev, z):
        return pl.ds(pl.multiple_of(dev * rows + z * piece, piece), piece)

    def remote(src, dst, send, recv, dp, blk):
        return pltpu.make_async_remote_copy(
            src_ref=src, dst_ref=dst, send_sem=send, recv_sem=recv,
            device_id=(dp, blk), device_id_type=MESH,
        )

    own = dev_rows(d)
    loads = [
        pltpu.make_async_copy(caps_hbm, caps.at[own], load_sem.at[0]),
        pltpu.make_async_copy(img_hbm, img.at[pl.ds(pl.multiple_of(b * per, per), per)], load_sem.at[1]),
        pltpu.make_async_copy(win_hbm, win, load_sem.at[2]),
        pltpu.make_async_copy(wout_hbm, wout, load_sem.at[3]),
    ]
    for load in loads:
        load.start()

    barrier = pltpu.get_barrier_semaphore()
    for k in range(1, nb):
        pl.semaphore_signal(barrier, inc=1, device_id=(d, z_at(k)), device_id_type=MESH)
    for k in range(1, nc):
        pl.semaphore_signal(barrier, inc=1, device_id=(chip_at(k) * 2 + core, b), device_id_type=MESH)
    pl.semaphore_signal(barrier, inc=1, device_id=(sibling, b), device_id_type=MESH)

    columns = lax.broadcasted_iota(jnp.int32, (outs, width), 1)
    lines = lax.broadcasted_iota(jnp.int32, (outs, width), 0)
    pick[...] = (columns == lines + d * outs).astype(jnp.float32).astype(jnp.bfloat16)

    pl.semaphore_wait(barrier, nb + nc - 1)

    started = []
    half_rows = pl.ds(pl.multiple_of(b * per + core * half, half), half)
    loads[1].wait()
    for k in range(1, nb):
        started.append(remote(img.at[half_rows], img.at[half_rows], img_send.at[k], img_recv.at[k], d, z_at(k)))
        started[-1].start()
    loads[0].wait()
    for k in range(1, nc):
        started.append(
            remote(caps.at[own], caps.at[own], cap_send.at[k], cap_recv.at[k], chip_at(k) * 2 + core, b)
        )
        started[-1].start()
    started.append(remote(caps.at[own], caps.at[own], cap_fsend.at[0], cap_frecv.at[0], sibling, b))
    started[-1].start()

    def forward_rows(block):
        @pl.loop(0, ff // CHUNK)
        def _(j):
            cols = pl.ds(pl.multiple_of(j * CHUNK, CHUNK), CHUNK)
            pre = jnp.dot(caps[block, :], win[:, cols], preferred_element_type=jnp.float32)
            h, s = gelu_and_slope(pre)
            hidden[block, cols] = h.astype(jnp.bfloat16)
            slope[block, cols] = s

    loads[2].wait()
    forward_rows(own)
    loads[3].wait()
    part[...] = jnp.dot(hidden[own, :], wout[...], preferred_element_type=jnp.float32)
    rs_send[...] = part[...].astype(jnp.bfloat16)
    for k in range(1, nb):
        away = pl.ds(pl.multiple_of(z_at(k) * piece, piece), piece)
        started.append(remote(rs_send.at[away], rs_recv.at[k], rs_ssem.at[k], rs_rsem.at[k], d, z_at(k)))
        started[-1].start()

    for k in range(1, nb):
        came = pl.ds(pl.multiple_of(z_from(k) * per + core * half, half), half)
        remote(img.at[came], img.at[came], img_send.at[k], img_recv.at[k], d, z_at(k)).wait_recv()
        started.append(remote(img.at[came], img.at[came], img_fsend.at[k], img_frecv.at[k], sibling, b))
        started[-1].start()
    for k in range(1, nb):
        came = pl.ds(pl.multiple_of(z_from(k) * per + (1 - core) * half, half), half)
        remote(img.at[came], img.at[came], img_fsend.at[k], img_frecv.at[k], sibling, b).wait_recv()
    raw = img[...].astype(jnp.float32)
    imgu[...] = (raw * lax.rsqrt(jnp.sum(raw * raw, axis=1, keepdims=True) + EPSILON)).astype(jnp.bfloat16)

    score_shape = (piece, nb * per)
    label_col = lax.broadcasted_iota(jnp.int32, score_shape, 1)
    label_row = lax.broadcasted_iota(jnp.int32, score_shape, 0)
    wanted = jnp.zeros(score_shape, jnp.int32)
    for i in range(piece):
        wanted = jnp.where(label_row == i, pairs[b * piece + i], wanted)
    labels = (label_col == wanted).astype(jnp.float32)

    embedding = part[pl.ds(pl.multiple_of(b * piece, piece), piece), :]
    for k in range(1, nb):
        remote(rs_send.at[pl.ds(0, piece)], rs_recv.at[k], rs_ssem.at[k], rs_rsem.at[k], d, z_at(k)).wait_recv()
        embedding = embedding + rs_recv[k].astype(jnp.float32)
    inv_norm = lax.rsqrt(jnp.sum(embedding * embedding, axis=1, keepdims=True) + EPSILON)
    unit = embedding * inv_norm
    logits = SCORE_SCALE * lax.dot_general(
        unit.astype(jnp.bfloat16), imgu[...], NT, preferred_element_type=jnp.float32
    ) + SCORE_BIAS_TERM
    mismatch = (1.0 / (1.0 + jnp.exp(-logits)) - labels).astype(jnp.bfloat16)
    unit_grad = SCORE_SCALE * jnp.dot(mismatch, imgu[...], preferred_element_type=jnp.float32)
    embed_grad = (unit_grad - unit * jnp.sum(unit * unit_grad, axis=1, keepdims=True)) * inv_norm
    mine = piece_rows(d, b)
    emb[mine, :] = embed_grad.astype(jnp.bfloat16)

    def spread(z, kz):
        src = emb.at[piece_rows(d, z)]
        for k in range(1, nc):
            started.append(
                remote(src, src, ex_send.at[k, kz], ex_recv.at[k, kz], chip_at(k) * 2 + core, b)
            )
            started[-1].start()
        started.append(remote(src, src, ef_send.at[0, kz], ef_recv.at[0, kz], sibling, b))
        started[-1].start()

    for k in range(1, nb):
        started.append(remote(emb.at[mine], emb.at[mine], ez_send.at[k], ez_recv.at[k], d, z_at(k)))
        started[-1].start()
    spread(b, 0)
    for kz in range(1, nb):
        src = emb.at[piece_rows(d, z_from(kz))]
        remote(src, src, ez_send.at[kz], ez_recv.at[kz], d, z_at(kz)).wait_recv()
        spread(z_from(kz), kz)

    for k in range(1, nc):
        src = caps.at[dev_rows(chip_from(k) * 2 + core)]
        remote(src, src, cap_send.at[k], cap_recv.at[k], chip_at(k) * 2 + core, b).wait_recv()
        started.append(remote(src, src, cap_fsend.at[k], cap_frecv.at[k], sibling, b))
        started[-1].start()
    for k in range(nc):
        other = caps.at[dev_rows(chip_from(k) * 2 + (1 - core))]
        remote(other, other, cap_fsend.at[k], cap_frecv.at[k], sibling, b).wait_recv()
        if k == 0:
            forward_rows(dev_rows(sibling))
        else:
            forward_rows(chip_rows(chip_from(k)))
        caps_t[:, chip_rows(chip_from(k))] = lax.dot_general(
            pick[...], caps[chip_rows(chip_from(k)), :], NT, preferred_element_type=jnp.float32
        ).astype(jnp.bfloat16)

    for kz in range(nb):
        for k in range(1, nc):
            src = emb.at[piece_rows(chip_from(k) * 2 + core, z_from(kz))]
            remote(src, src, ex_send.at[k, kz], ex_recv.at[k, kz], chip_at(k) * 2 + core, b).wait_recv()
            started.append(remote(src, src, ef_send.at[k, kz], ef_recv.at[k, kz], sibling, b))
            started[-1].start()
    for k in range(nc):
        for kz in range(nb):
            src = emb.at[piece_rows(chip_from(k) * 2 + (1 - core), z_from(kz))]
            remote(src, src, ef_send.at[k, kz], ef_recv.at[k, kz], sibling, b).wait_recv()
        block = chip_rows(chip_from(k))
        emb_t[:, block] = lax.dot_general(
            pick[...], emb[block, :], NT, preferred_element_type=jnp.float32
        ).astype(jnp.bfloat16)

        @pl.loop(0, ff // CHUNK)
        def _(j):
            cols = pl.ds(pl.multiple_of(j * CHUNK, CHUNK), CHUNK)
            back = lax.dot_general(emb[block, :], wout[cols, :], NT, preferred_element_type=jnp.float32)
            pgrad[block, cols] = (back * slope[block, cols]).astype(jnp.bfloat16)

    def product(left, right, out):
        @pl.loop(0, ff // CHUNK)
        def _(j):
            cols = pl.ds(pl.multiple_of(j * CHUNK, CHUNK), CHUNK)
            out[:, cols] = jnp.dot(left[...], right[:, cols], preferred_element_type=jnp.float32)

    product(emb_t, hidden, gout)
    store_out = pltpu.make_async_copy(gout, gout_hbm, store_sem.at[0])
    store_out.start()
    product(caps_t, pgrad, gin)
    store_in = pltpu.make_async_copy(gin, gin_hbm, store_sem.at[1])
    store_in.start()
    for copy in started:
        copy.wait_send()
    store_out.wait()
    store_in.wait()


def fused_body(nd, nb, captions, w_in, w_out, images, pairs):
    rows, width = captions.shape
    ff = w_in.shape[1]
    per = images.shape[0]
    piece = rows // nb
    outs = width // nd
    nc = nd // 2
    half, single = jnp.bfloat16, jnp.float32
    dma = pltpu.SemaphoreType.DMA
    vmem = pltpu.VMEM
    anywhere = pl.BlockSpec(memory_space=pl.ANY)
    return pl.pallas_call(
        functools.partial(head_kernel, nd, nb),
        out_shape=[jax.ShapeDtypeStruct((outs, ff), single)] * 2,
        in_specs=[anywhere] * 4 + [pl.BlockSpec(memory_space=pltpu.SMEM)],
        out_specs=[anywhere] * 2,
        scratch_shapes=[
            vmem((width, ff), half),
            vmem((ff, width), half),
            vmem((nb * per, width), half),
            vmem((nb * per, width), half),
            vmem((nd * rows, width), half),
            vmem((nd * rows, width), half),
            vmem((rows, width), single),
            vmem((rows, width), half),
            vmem((nb, piece, width), half),
            vmem((nd * rows, ff), half),
            vmem((nd * rows, ff), single),
            vmem((nd * rows, ff), half),
            vmem((outs, width), half),
            vmem((outs, nd * rows), half),
            vmem((outs, nd * rows), half),
            vmem((outs, ff), single),
            vmem((outs, ff), single),
            dma((4,)),
            dma((2,)),
            dma((nc,)), dma((nc,)), dma((nc,)), dma((nc,)),
            dma((nb,)), dma((nb,)), dma((nb,)), dma((nb,)),
            dma((nb,)), dma((nb,)),
            dma((nb,)), dma((nb,)),
            dma((nc, nb)), dma((nc, nb)), dma((nc, nb)), dma((nc, nb)),
        ],
        compiler_params=pltpu.CompilerParams(
            collective_id=0, has_side_effects=True, vmem_limit_bytes=VMEM_BYTES
        ),
    )(captions, w_in, w_out, images, pairs)


def fits(nd, nb, captions, w_in, images):
    rows, width = captions.shape
    ff = w_in.shape[1]
    per = images.shape[0]
    scratch = (
        4 * width * ff
        + 4 * nb * per * width
        + 4 * nd * rows * width
        + 16 * rows * width
        + 8 * nd * rows * ff
        + 8 * (width // nd) * ff
    )
    return (
        nd % 2 == 0
        and nb > 1
        and nd > 2
        and ff % CHUNK == 0
        and rows % (16 * nb) == 0
        and (2 * rows) % 128 == 0
        and per % 32 == 0
        and width % (16 * nd) == 0
        and scratch < VMEM_BYTES * 3 // 4
    )


def body(captions, w_in, w_out, images, pairs):
    nd, nb = lax.axis_size("dp"), lax.axis_size("blk")
    if fits(nd, nb, captions, w_in, images):
        return tuple(fused_body(nd, nb, captions, w_in, w_out, images, pairs))
    return staged_body(captions, w_in, w_out, images, pairs)


def solution(mesh):
    return jax.shard_map(
        body,
        mesh=mesh,
        in_specs=(P("dp", None), P(None, "blk"), P("blk", None), P("blk", None), P("dp")),
        out_specs=(P("dp", "blk"), P("dp", "blk")),
        check_vma=False,
    )
```

```python
import functools

import jax
import jax.numpy as jnp
from jax import lax
from jax.experimental import pallas as pl
from jax.experimental.pallas import tpu as pltpu
from jax.sharding import PartitionSpec as P

SCORE_SCALE = 10.0
SCORE_BIAS_TERM = -5.0
EPSILON = 1e-06


def from_behind(block, axis, distance):
    devices = range(lax.axis_size(axis))
    route = [((i - distance) % len(devices), i) for i in devices]
    return lax.ppermute(block, axis, route)


def activate(values):
    return jax.nn.gelu(values, approximate=True)


def tile_grad(direction_halfway, image_direction, first_image, row_pairs):
    pair_scores = (
        SCORE_SCALE
        * lax.dot_general(
            direction_halfway,
            image_direction,
            (((1,), (1,)), ((), ())),
            preferred_element_type=jnp.float32,
        )
        + SCORE_BIAS_TERM
    )
    columns = first_image + lax.broadcasted_iota(jnp.int32, pair_scores.shape, 1)
    labels = (row_pairs[:, None] == columns).astype(jnp.float32)
    label_error = (jax.nn.sigmoid(pair_scores) - labels).astype(jnp.bfloat16)
    return SCORE_SCALE * jnp.dot(label_error, image_direction, preferred_element_type=jnp.float32)


def staged_body(captions, w_in, w_out, images, pairs):
    cycle_size = lax.axis_size("blk")
    cycle_pos = lax.axis_index("blk")
    own_rows = captions.shape[0] // cycle_size
    block_len = images.shape[0]
    width = captions.shape[1]
    pre_act = jnp.dot(captions, w_in, preferred_element_type=jnp.float32)
    hidden = activate(pre_act).astype(jnp.bfloat16)
    rows_hidden = hidden
    embedding = lax.psum_scatter(
        jnp.dot(rows_hidden, w_out, preferred_element_type=jnp.float32),
        "blk",
        scatter_dimension=0,
        tiled=True,
    )
    inv_norm = lax.rsqrt(jnp.sum(embedding * embedding, axis=1, keepdims=True) + EPSILON)
    unit_dir = embedding * inv_norm
    direction_halfway = unit_dir.astype(jnp.bfloat16)
    image_vals = images.astype(jnp.float32)
    image_direction = (
        image_vals * lax.rsqrt(jnp.sum(image_vals * image_vals, axis=1, keepdims=True) + EPSILON)
    ).astype(jnp.bfloat16)
    row_pairs = lax.dynamic_slice_in_dim(pairs, cycle_pos * own_rows, own_rows, 0)

    def visit(step, carry):
        running, block = carry
        source = (cycle_pos - step) % cycle_size
        running = running + tile_grad(direction_halfway, block, source * block_len, row_pairs)
        block = from_behind(block, "blk", 1)
        return (running, block)

    start_sum = jnp.zeros((own_rows, width), jnp.float32)
    running, block = lax.fori_loop(0, cycle_size - 1, visit, (start_sum, image_direction))
    source = (cycle_pos - (cycle_size - 1)) % cycle_size
    direction_gradient = running + tile_grad(
        direction_halfway, block, source * block_len, row_pairs
    )
    embed_grad = (
        direction_gradient
        - unit_dir * jnp.sum(unit_dir * direction_gradient, axis=1, keepdims=True)
    ) * inv_norm
    embed_half = embed_grad.astype(jnp.bfloat16)
    piece = lax.all_gather(embed_half, "blk", axis=0, tiled=True)
    rows_hidden = hidden
    hidden_grad = lax.dot_general(
        piece, w_out, (((1,), (1,)), ((), ())), preferred_element_type=jnp.float32
    )
    _, pullback = jax.vjp(activate, pre_act)
    preact_grad = pullback(hidden_grad)[0].astype(jnp.bfloat16)
    grad_in = lax.dot_general(
        captions, preact_grad, (((0,), (0,)), ((), ())), preferred_element_type=jnp.float32
    )
    grad_out = lax.dot_general(
        piece, rows_hidden, (((0,), (0,)), ((), ())), preferred_element_type=jnp.float32
    )
    grad_in, grad_out = (grad_in, grad_out)
    grad_w_in, grad_w_out_t = (
        lax.psum_scatter(grad_in, "dp", scatter_dimension=0, tiled=True),
        lax.psum_scatter(grad_out, "dp", scatter_dimension=0, tiled=True),
    )
    return (grad_w_in, grad_w_out_t)


MESH = pl.DeviceIdType.MESH
CHUNK = 256
WIDE = 512
VMEM_BYTES = 60 * 2**20
GELU_SCALE = 0.7978845608028654
GELU_CUBE = 0.044715
NT = (((1,), (1,)), ((), ()))


def gelu_and_slope(v):
    square = v * v
    t = jnp.tanh(GELU_SCALE * (v + GELU_CUBE * (square * v)))
    half = 0.5 * (1.0 + t)
    slope = half + (0.5 * GELU_SCALE) * v * (1.0 - t * t) * (1.0 + (3.0 * GELU_CUBE) * square)
    return v * half, slope


def head_kernel(
    nd, nb,
    caps_hbm, win_hbm, wout_hbm, img_hbm, pairs, hidden_hbm, pgrad_hbm, capst_hbm, embt_hbm,
    win, wout, wout_t, img, imgu, caps, emb, part, rs_send, rs_recv, hidden, slope, pgrad,
    pick, caps_t, emb_t,
    load_sem, store_sem,
    cap_send, cap_recv, cap_dsend, cap_drecv, cap_fsend, cap_frecv,
    img_send, img_recv, img_xsend, img_xrecv, img_fsend, img_frecv,
    rs_ssem, rs_rsem,
    ez_send, ez_recv, ex_send, ex_recv, ed_send, ed_recv, ef_send, ef_recv,
):
    d = lax.axis_index("dp")
    b = lax.axis_index("blk")
    core = d % 2
    chip = d // 2
    chips = (chip, chip + 1 - 2 * (chip % 2), (chip + 2) % 4, 3 - chip)
    sibling = chip * 2 + (1 - core)
    rows, width = caps_hbm.shape
    ff = win_hbm.shape[1]
    per = img_hbm.shape[0]
    half = per // 2
    piece = rows // nb

    def z_at(k):
        return (b + k) % nb

    def z_from(k):
        return (b + nb - k) % nb

    def peer(r):
        return chips[r] * 2 + core

    def other(r):
        return chips[r] * 2 + (1 - core)

    def dev_rows(dev, part=0, parts=1):
        size = rows // parts
        return pl.ds(pl.multiple_of(dev * rows + part * size, size), size)

    def chip_rows(c):
        return pl.ds(pl.multiple_of(c * (2 * rows), 2 * rows), 2 * rows)

    def piece_rows(dev, z):
        return pl.ds(pl.multiple_of(dev * rows + z * piece, piece), piece)

    def image_rows(c, side):
        return pl.ds(pl.multiple_of(z_from(c) * per + side * half, half), half)

    def remote(ref, where, send, recv, dp, blk=b):
        return pltpu.make_async_remote_copy(
            src_ref=ref.at[where], dst_ref=ref.at[where], send_sem=send, recv_sem=recv,
            device_id=(dp, blk), device_id_type=MESH,
        )

    started = []

    def send(copy):
        copy.start()
        started.append(copy)

    own = dev_rows(d)
    own_images = pl.ds(pl.multiple_of(b * per, per), per)
    loads = [
        pltpu.make_async_copy(caps_hbm, caps.at[own], load_sem.at[0]),
        pltpu.make_async_copy(win_hbm, win, load_sem.at[1]),
        pltpu.make_async_copy(wout_hbm, wout, load_sem.at[2]),
        pltpu.make_async_copy(img_hbm, img.at[own_images], load_sem.at[3]),
    ]
    for load in loads:
        load.start()

    barrier = pltpu.get_barrier_semaphore()
    for k in range(1, nb):
        pl.semaphore_signal(barrier, inc=1, device_id=(d, z_at(k)), device_id_type=MESH)
    for r in (1, 2, 3):
        pl.semaphore_signal(barrier, inc=1, device_id=(peer(r), b), device_id_type=MESH)
    pl.semaphore_signal(barrier, inc=1, device_id=(sibling, b), device_id_type=MESH)

    def forward(source, target):
        @pl.loop(0, ff // CHUNK)
        def _(j):
            cols = pl.ds(pl.multiple_of(j * CHUNK, CHUNK), CHUNK)
            pre = jnp.dot(caps[source, :], win[:, cols], preferred_element_type=jnp.float32)
            h, s = gelu_and_slope(pre)
            hidden[target, cols] = h.astype(jnp.bfloat16)
            slope[target, cols] = s

    def near(side):
        return pl.ds(pl.multiple_of(side * rows, rows), rows)

    def far(r):
        return pl.ds(r * 2 * rows, 2 * rows)

    loads[0].wait()
    loads[1].wait()
    forward(own, near(core))
    loads[2].wait()
    part[...] = jnp.dot(hidden[near(core), :], wout[...], preferred_element_type=jnp.float32)
    rs_send[...] = part[...].astype(jnp.bfloat16)
    loads[3].wait()

    pl.semaphore_wait(barrier, nb + 3)

    def rs_copy(k):
        away = pl.ds(pl.multiple_of(z_at(k) * piece, piece), piece)
        return pltpu.make_async_remote_copy(
            src_ref=rs_send.at[away], dst_ref=rs_recv.at[k], send_sem=rs_ssem.at[k],
            recv_sem=rs_rsem.at[k], device_id=(d, z_at(k)), device_id_type=MESH,
        )

    def brings(c):
        return (c > 0) & (c < nb)

    def image_z(where):
        return remote(img, where, img_send.at[0], img_recv.at[0], d, (b + chip) % nb)

    @pl.when(brings(chip))
    def _():
        image_z(image_rows(0, core)).start()

    for k in range(1, nb):
        send(rs_copy(k))
    send(remote(caps, own, cap_fsend.at[0], cap_frecv.at[0], sibling))
    for r in (1, 2):
        send(remote(caps, own, cap_send.at[r], cap_recv.at[r], peer(r)))

    columns = lax.broadcasted_iota(jnp.int32, pick.shape, 1)
    lines = lax.broadcasted_iota(jnp.int32, pick.shape, 0)
    pick[...] = (columns == lines + d * pick.shape[0]).astype(jnp.float32).astype(jnp.bfloat16)

    remote(caps, dev_rows(sibling), cap_fsend.at[0], cap_frecv.at[0], sibling).wait_recv()
    forward(dev_rows(sibling), near(1 - core))

    def image_x(r, where):
        return remote(img, where, img_xsend.at[r], img_xrecv.at[r], peer(r))

    def image_f(r, where):
        return remote(img, where, img_fsend.at[r], img_frecv.at[r], sibling)

    @pl.when(brings(chip))
    def _():
        came = image_rows(chip, core)
        image_z(came).wait_recv()
        for r in (1, 2, 3):
            image_x(r, came).start()
        image_f(0, came).start()

    @pl.loop(0, ff // CHUNK)
    def _(j):
        cols = pl.ds(pl.multiple_of(j * CHUNK, CHUNK), CHUNK)
        wout_t[:, cols] = wout[cols, :].T

    for r in (1, 2, 3):
        @pl.when(brings(chips[r]))
        def _():
            came = image_rows(chips[r], core)
            image_x(r, came).wait_recv()
            image_f(r, came).start()

    for r in (1, 2):
        remote(caps, dev_rows(peer(r)), cap_send.at[r], cap_recv.at[r], peer(r)).wait_recv()
        send(remote(caps, dev_rows(peer(r), r - 1, 2), cap_dsend.at[r - 1], cap_drecv.at[r - 1], peer(3 - r)))
        send(remote(caps, dev_rows(peer(r)), cap_fsend.at[r], cap_frecv.at[r], sibling))

    for r in range(4):
        @pl.when(brings(chips[r]))
        def _():
            image_f(r, image_rows(chips[r], 1 - core)).wait_recv()
    raw = img[...].astype(jnp.float32)
    imgu[...] = (raw * lax.rsqrt(jnp.sum(raw * raw, axis=1, keepdims=True) + EPSILON)).astype(jnp.bfloat16)

    score_shape = (piece, nb * per)
    label_col = lax.broadcasted_iota(jnp.int32, score_shape, 1)
    label_row = lax.broadcasted_iota(jnp.int32, score_shape, 0)
    wanted = jnp.zeros(score_shape, jnp.int32)
    for i in range(piece):
        wanted = jnp.where(label_row == i, pairs[b * piece + i], wanted)
    labels = (label_col == wanted).astype(jnp.float32)

    embedding = part[pl.ds(pl.multiple_of(b * piece, piece), piece), :]
    for k in range(1, nb):
        rs_copy(k).wait_recv()
        embedding = embedding + rs_recv[k].astype(jnp.float32)
    inv_norm = lax.rsqrt(jnp.sum(embedding * embedding, axis=1, keepdims=True) + EPSILON)
    unit = embedding * inv_norm
    logits = SCORE_SCALE * lax.dot_general(
        unit.astype(jnp.bfloat16), imgu[...], NT, preferred_element_type=jnp.float32
    ) + SCORE_BIAS_TERM
    mismatch = (1.0 / (1.0 + jnp.exp(-logits)) - labels).astype(jnp.bfloat16)
    unit_grad = SCORE_SCALE * jnp.dot(mismatch, imgu[...], preferred_element_type=jnp.float32)
    embed_grad = (unit_grad - unit * jnp.sum(unit * unit_grad, axis=1, keepdims=True)) * inv_norm
    mine = piece_rows(d, b)
    emb[mine, :] = embed_grad.astype(jnp.bfloat16)

    def ez_copy(kz, where):
        return remote(emb, where, ez_send.at[kz], ez_recv.at[kz], d, z_at(kz))

    def ex_copy(r, kz, dev):
        return remote(emb, piece_rows(dev, z_from(kz)), ex_send.at[r, kz], ex_recv.at[r, kz], peer(r))

    def ed_copy(kz, dev):
        over = 1 if kz < nb // 2 else 2
        return remote(emb, piece_rows(dev, z_from(kz)), ed_send.at[kz], ed_recv.at[kz], peer(3 - over))

    def ef_copy(r, kz, dev):
        return remote(emb, piece_rows(dev, z_from(kz)), ef_send.at[r, kz], ef_recv.at[r, kz], sibling)

    for kz in range(1, nb):
        send(ez_copy(kz, mine))

    def spread(kz):
        for r in (1, 2):
            send(ex_copy(r, kz, d))
        send(ef_copy(0, kz, d))

    def relay(kz):
        over = 1 if kz < nb // 2 else 2
        for r in (over, 3 - over):
            ex_copy(r, kz, peer(r)).wait_recv()
            if r == over:
                send(ed_copy(kz, peer(r)))
            send(ef_copy(r, kz, peer(r)))

    def forward_chip(r):
        if r:
            forward(chip_rows(chips[r]), far(r))
        caps_t[:, far(r)] = lax.dot_general(
            pick[...], caps[chip_rows(chips[r]), :], NT, preferred_element_type=jnp.float32
        ).astype(jnp.bfloat16)

    stores = []

    def store(src, dst):
        stores.append(pltpu.make_async_copy(src, dst, store_sem.at[len(stores)]))
        stores[-1].start()

    def backward_chip(r):
        for kz in range(nb):
            ef_copy(r, kz, other(r)).wait_recv()

        @pl.loop(0, ff // CHUNK)
        def _(j):
            cols = pl.ds(pl.multiple_of(j * CHUNK, CHUNK), CHUNK)
            back = jnp.dot(emb[chip_rows(chips[r]), :], wout_t[:, cols], preferred_element_type=jnp.float32)
            pgrad[far(r), cols] = (back * slope[far(r), cols]).astype(jnp.bfloat16)

        store(pgrad.at[far(r)], pgrad_hbm.at[far(r)])
        emb_t[:, far(r)] = lax.dot_general(
            pick[...], emb[chip_rows(chips[r]), :], NT, preferred_element_type=jnp.float32
        ).astype(jnp.bfloat16)

    spread(0)
    remote(caps, dev_rows(other(1)), cap_fsend.at[1], cap_frecv.at[1], sibling).wait_recv()
    forward_chip(1)
    for kz in range(1, nb + 1):
        if kz < nb:
            ez_copy(kz, piece_rows(d, z_from(kz))).wait_recv()
            spread(kz)
        relay(kz - 1)

    for h in (0, 1):
        across = dev_rows(peer(3), h, 2)
        remote(caps, across, cap_dsend.at[h], cap_drecv.at[h], peer(2 - h)).wait_recv()
        send(remote(caps, across, cap_fsend.at[3 + h], cap_frecv.at[3 + h], sibling))
    remote(caps, dev_rows(other(2)), cap_fsend.at[2], cap_frecv.at[2], sibling).wait_recv()
    forward_chip(0)
    forward_chip(2)
    backward_chip(0)
    for kz in range(nb):
        ed_copy(kz, peer(3)).wait_recv()
        send(ef_copy(3, kz, peer(3)))
    for h in (0, 1):
        across = dev_rows(other(3), h, 2)
        remote(caps, across, cap_fsend.at[3 + h], cap_frecv.at[3 + h], sibling).wait_recv()
    forward_chip(3)
    store(hidden, hidden_hbm)
    store(caps_t, capst_hbm)
    backward_chip(1)
    backward_chip(2)
    backward_chip(3)
    store(emb_t, embt_hbm)

    @pl.when(brings(chip))
    def _():
        image_z(image_rows(0, core)).wait_send()
        came = image_rows(chip, core)
        for r in (1, 2, 3):
            image_x(r, came).wait_send()
        image_f(0, came).wait_send()

    for r in (1, 2, 3):
        @pl.when(brings(chips[r]))
        def _():
            image_f(r, image_rows(chips[r], core)).wait_send()

    for copy in started:
        copy.wait_send()
    for copy in stores:
        copy.wait()


def product_kernel(caps_t, pgrad, emb_t, hidden, gin, gout):
    gin[...] = jnp.dot(caps_t[...], pgrad[...], preferred_element_type=jnp.float32)
    gout[...] = jnp.dot(emb_t[...], hidden[...], preferred_element_type=jnp.float32)


def fused_body(nd, nb, captions, w_in, w_out, images, pairs):
    rows, width = captions.shape
    ff = w_in.shape[1]
    per = images.shape[0]
    piece = rows // nb
    outs = width // nd
    half, single = jnp.bfloat16, jnp.float32
    dma = pltpu.SemaphoreType.DMA
    vmem = pltpu.VMEM
    anywhere = pl.BlockSpec(memory_space=pl.ANY)
    hidden, pgrad, caps_t, emb_t = pl.pallas_call(
        functools.partial(head_kernel, nd, nb),
        out_shape=[
            jax.ShapeDtypeStruct((nd * rows, ff), half),
            jax.ShapeDtypeStruct((nd * rows, ff), half),
            jax.ShapeDtypeStruct((outs, nd * rows), half),
            jax.ShapeDtypeStruct((outs, nd * rows), half),
        ],
        in_specs=[anywhere] * 4 + [pl.BlockSpec(memory_space=pltpu.SMEM)],
        out_specs=[anywhere] * 4,
        scratch_shapes=[
            vmem((width, ff), half),
            vmem((ff, width), half),
            vmem((width, ff), half),
            vmem((nb * per, width), half),
            vmem((nb * per, width), half),
            vmem((nd * rows, width), half),
            vmem((nd * rows, width), half),
            vmem((rows, width), single),
            vmem((rows, width), half),
            vmem((nb, piece, width), half),
            vmem((nd * rows, ff), half),
            vmem((nd * rows, ff), single),
            vmem((nd * rows, ff), half),
            vmem((outs, width), half),
            vmem((outs, nd * rows), half),
            vmem((outs, nd * rows), half),
            dma((4,)),
            dma((7,)),
            dma((3,)), dma((3,)), dma((2,)), dma((2,)), dma((5,)), dma((5,)),
            dma((1,)), dma((1,)), dma((4,)), dma((4,)), dma((4,)), dma((4,)),
            dma((nb,)), dma((nb,)),
            dma((nb,)), dma((nb,)), dma((3, nb)), dma((3, nb)),
            dma((nb,)), dma((nb,)), dma((4, nb)), dma((4, nb)),
        ],
        compiler_params=pltpu.CompilerParams(
            collective_id=0, has_side_effects=True, vmem_limit_bytes=VMEM_BYTES
        ),
    )(captions, w_in, w_out, images, pairs)
    left = pl.BlockSpec((outs, nd * rows), lambda j: (0, 0))
    right = pl.BlockSpec((nd * rows, WIDE), lambda j: (0, j))
    result = pl.BlockSpec((outs, WIDE), lambda j: (0, j))
    return pl.pallas_call(
        product_kernel,
        grid=(ff // WIDE,),
        out_shape=[jax.ShapeDtypeStruct((outs, ff), single)] * 2,
        in_specs=[left, right, left, right],
        out_specs=[result] * 2,
        compiler_params=pltpu.CompilerParams(vmem_limit_bytes=VMEM_BYTES),
    )(caps_t, pgrad, emb_t, hidden)


def fits(nd, nb, captions, w_in, images):
    rows, width = captions.shape
    ff = w_in.shape[1]
    per = images.shape[0]
    scratch = (
        6 * width * ff
        + 4 * nb * per * width
        + 4 * nd * rows * width
        + 16 * rows * width
        + 8 * nd * rows * ff
    )
    return (
        nd == 8
        and 1 < nb <= 4
        and ff % CHUNK == 0
        and ff % WIDE == 0
        and rows % (16 * nb) == 0
        and rows % 64 == 0
        and per % 32 == 0
        and width % (16 * nd) == 0
        and scratch < VMEM_BYTES * 3 // 4
    )


def body(captions, w_in, w_out, images, pairs):
    nd, nb = lax.axis_size("dp"), lax.axis_size("blk")
    if fits(nd, nb, captions, w_in, images):
        return tuple(fused_body(nd, nb, captions, w_in, w_out, images, pairs))
    return staged_body(captions, w_in, w_out, images, pairs)


def solution(mesh):
    return jax.shard_map(
        body,
        mesh=mesh,
        in_specs=(P("dp", None), P(None, "blk"), P("blk", None), P("blk", None), P("dp")),
        out_specs=(P("dp", "blk"), P("dp", "blk")),
        check_vma=False,
    )
```

```python
import functools

import jax
import jax.numpy as jnp
from jax import lax
from jax.experimental import pallas as pl
from jax.experimental.pallas import tpu as pltpu
from jax.sharding import PartitionSpec as P

SCORE_SCALE = 10.0
SCORE_BIAS_TERM = -5.0
EPSILON = 1e-06


def from_behind(block, axis, distance):
    devices = range(lax.axis_size(axis))
    route = [((i - distance) % len(devices), i) for i in devices]
    return lax.ppermute(block, axis, route)


def activate(values):
    return jax.nn.gelu(values, approximate=True)


def tile_grad(direction_halfway, image_direction, first_image, row_pairs):
    pair_scores = (
        SCORE_SCALE
        * lax.dot_general(
            direction_halfway,
            image_direction,
            (((1,), (1,)), ((), ())),
            preferred_element_type=jnp.float32,
        )
        + SCORE_BIAS_TERM
    )
    columns = first_image + lax.broadcasted_iota(jnp.int32, pair_scores.shape, 1)
    labels = (row_pairs[:, None] == columns).astype(jnp.float32)
    label_error = (jax.nn.sigmoid(pair_scores) - labels).astype(jnp.bfloat16)
    return SCORE_SCALE * jnp.dot(label_error, image_direction, preferred_element_type=jnp.float32)


def staged_body(captions, w_in, w_out, images, pairs):
    cycle_size = lax.axis_size("blk")
    cycle_pos = lax.axis_index("blk")
    own_rows = captions.shape[0] // cycle_size
    block_len = images.shape[0]
    width = captions.shape[1]
    pre_act = jnp.dot(captions, w_in, preferred_element_type=jnp.float32)
    hidden = activate(pre_act).astype(jnp.bfloat16)
    rows_hidden = hidden
    embedding = lax.psum_scatter(
        jnp.dot(rows_hidden, w_out, preferred_element_type=jnp.float32),
        "blk",
        scatter_dimension=0,
        tiled=True,
    )
    inv_norm = lax.rsqrt(jnp.sum(embedding * embedding, axis=1, keepdims=True) + EPSILON)
    unit_dir = embedding * inv_norm
    direction_halfway = unit_dir.astype(jnp.bfloat16)
    image_vals = images.astype(jnp.float32)
    image_direction = (
        image_vals * lax.rsqrt(jnp.sum(image_vals * image_vals, axis=1, keepdims=True) + EPSILON)
    ).astype(jnp.bfloat16)
    row_pairs = lax.dynamic_slice_in_dim(pairs, cycle_pos * own_rows, own_rows, 0)

    def visit(step, carry):
        running, block = carry
        source = (cycle_pos - step) % cycle_size
        running = running + tile_grad(direction_halfway, block, source * block_len, row_pairs)
        block = from_behind(block, "blk", 1)
        return (running, block)

    start_sum = jnp.zeros((own_rows, width), jnp.float32)
    running, block = lax.fori_loop(0, cycle_size - 1, visit, (start_sum, image_direction))
    source = (cycle_pos - (cycle_size - 1)) % cycle_size
    direction_gradient = running + tile_grad(
        direction_halfway, block, source * block_len, row_pairs
    )
    embed_grad = (
        direction_gradient
        - unit_dir * jnp.sum(unit_dir * direction_gradient, axis=1, keepdims=True)
    ) * inv_norm
    embed_half = embed_grad.astype(jnp.bfloat16)
    piece = lax.all_gather(embed_half, "blk", axis=0, tiled=True)
    rows_hidden = hidden
    hidden_grad = lax.dot_general(
        piece, w_out, (((1,), (1,)), ((), ())), preferred_element_type=jnp.float32
    )
    _, pullback = jax.vjp(activate, pre_act)
    preact_grad = pullback(hidden_grad)[0].astype(jnp.bfloat16)
    grad_in = lax.dot_general(
        captions, preact_grad, (((0,), (0,)), ((), ())), preferred_element_type=jnp.float32
    )
    grad_out = lax.dot_general(
        piece, rows_hidden, (((0,), (0,)), ((), ())), preferred_element_type=jnp.float32
    )
    grad_in, grad_out = (grad_in, grad_out)
    grad_w_in, grad_w_out_t = (
        lax.psum_scatter(grad_in, "dp", scatter_dimension=0, tiled=True),
        lax.psum_scatter(grad_out, "dp", scatter_dimension=0, tiled=True),
    )
    return (grad_w_in, grad_w_out_t)


MESH = pl.DeviceIdType.MESH
CHUNK = 256
WIDE = 512
VMEM_BYTES = 60 * 2**20
GELU_SCALE = 0.7978845608028654
GELU_CUBE = 0.044715
NT = (((1,), (1,)), ((), ()))


def gelu_and_slope(v):
    square = v * v
    t = jnp.tanh(GELU_SCALE * (v + GELU_CUBE * (square * v)))
    half = 0.5 * (1.0 + t)
    slope = half + (0.5 * GELU_SCALE) * v * (1.0 - t * t) * (1.0 + (3.0 * GELU_CUBE) * square)
    return v * half, slope


def head_kernel(
    nd, nb,
    caps_hbm, win_hbm, wout_hbm, img_hbm, pairs, hidden_hbm, pgrad_hbm, capst_hbm, embt_hbm,
    win, wout, wout_t, img, imgu, caps, emb, part, rs_send, rs_recv, hidden, slope, pgrad,
    pick, caps_t, emb_t,
    load_sem, store_sem,
    cap_send, cap_recv, cap_fsend, cap_frecv,
    img_send, img_recv, img_fsend, img_frecv,
    rs_ssem, rs_rsem,
    ez_send, ez_recv, ea_send, ea_recv, ex_send, ex_recv, ef_send, ef_recv,
):
    d = lax.axis_index("dp")
    b = lax.axis_index("blk")
    core = d % 2
    chip = d // 2
    chips = (chip, chip + 1 - 2 * (chip % 2), (chip + 2) % 4, 3 - chip)
    sibling = chip * 2 + (1 - core)
    rows, width = caps_hbm.shape
    ff = win_hbm.shape[1]
    per = img_hbm.shape[0]
    half = per // 2
    piece = rows // nb

    def z_at(k):
        return (b + k) % nb

    def z_from(k):
        return (b + nb - k) % nb

    def peer(r):
        return chips[r] * 2 + core

    def other(r):
        return chips[r] * 2 + (1 - core)

    def dev_rows(dev, part=0, parts=1):
        size = rows // parts
        return pl.ds(pl.multiple_of(dev * rows + part * size, size), size)

    def chip_rows(c):
        return pl.ds(pl.multiple_of(c * (2 * rows), 2 * rows), 2 * rows)

    def piece_rows(dev, z):
        return pl.ds(pl.multiple_of(dev * rows + z * piece, piece), piece)

    def image_rows(k, side):
        return pl.ds(pl.multiple_of(z_from(k) * per + side * half, half), half)

    def remote(ref, where, send, recv, dp, blk=b):
        return pltpu.make_async_remote_copy(
            src_ref=ref.at[where], dst_ref=ref.at[where], send_sem=send, recv_sem=recv,
            device_id=(dp, blk), device_id_type=MESH,
        )

    started = []

    def send(copy):
        copy.start()
        started.append(copy)

    own = dev_rows(d)
    own_images = pl.ds(pl.multiple_of(b * per, per), per)
    loads = [
        pltpu.make_async_copy(caps_hbm, caps.at[own], load_sem.at[0]),
        pltpu.make_async_copy(win_hbm, win, load_sem.at[1]),
        pltpu.make_async_copy(wout_hbm, wout, load_sem.at[2]),
        pltpu.make_async_copy(img_hbm, img.at[own_images], load_sem.at[3]),
    ]
    for load in loads:
        load.start()

    barrier = pltpu.get_barrier_semaphore()
    for k in range(1, nb):
        pl.semaphore_signal(barrier, inc=1, device_id=(d, z_at(k)), device_id_type=MESH)
    for r in (1, 2, 3):
        pl.semaphore_signal(barrier, inc=1, device_id=(peer(r), b), device_id_type=MESH)
    pl.semaphore_signal(barrier, inc=1, device_id=(sibling, b), device_id_type=MESH)

    def forward(source, target):
        @pl.loop(0, ff // CHUNK)
        def _(j):
            cols = pl.ds(pl.multiple_of(j * CHUNK, CHUNK), CHUNK)
            pre = jnp.dot(caps[source, :], win[:, cols], preferred_element_type=jnp.float32)
            h, s = gelu_and_slope(pre)
            hidden[target, cols] = h.astype(jnp.bfloat16)
            slope[target, cols] = s

    def near(side):
        return pl.ds(pl.multiple_of(side * rows, rows), rows)

    def far(r):
        return pl.ds(r * 2 * rows, 2 * rows)

    loads[0].wait()
    loads[1].wait()
    forward(own, near(core))
    loads[2].wait()
    part[...] = jnp.dot(hidden[near(core), :], wout[...], preferred_element_type=jnp.float32)
    rs_send[...] = part[...].astype(jnp.bfloat16)
    loads[3].wait()

    pl.semaphore_wait(barrier, nb + 3)

    def rs_copy(k):
        away = pl.ds(pl.multiple_of(z_at(k) * piece, piece), piece)
        return pltpu.make_async_remote_copy(
            src_ref=rs_send.at[away], dst_ref=rs_recv.at[k], send_sem=rs_ssem.at[k],
            recv_sem=rs_rsem.at[k], device_id=(d, z_at(k)), device_id_type=MESH,
        )

    def image_z(k, where):
        return remote(img, where, img_send.at[k], img_recv.at[k], d, z_at(k))

    def image_f(k, where):
        return remote(img, where, img_fsend.at[k], img_frecv.at[k], sibling)

    for k in range(1, nb):
        send(rs_copy(k))
    for k in range(1, nb):
        send(image_z(k, image_rows(0, core)))
    send(remote(caps, own, cap_fsend.at[0], cap_frecv.at[0], sibling))
    for r in (1, 2, 3):
        send(remote(caps, own, cap_send.at[r], cap_recv.at[r], peer(r)))

    columns = lax.broadcasted_iota(jnp.int32, pick.shape, 1)
    lines = lax.broadcasted_iota(jnp.int32, pick.shape, 0)
    pick[...] = (columns == lines + d * pick.shape[0]).astype(jnp.float32).astype(jnp.bfloat16)

    remote(caps, dev_rows(sibling), cap_fsend.at[0], cap_frecv.at[0], sibling).wait_recv()
    forward(dev_rows(sibling), near(1 - core))

    @pl.loop(0, ff // CHUNK)
    def _(j):
        cols = pl.ds(pl.multiple_of(j * CHUNK, CHUNK), CHUNK)
        wout_t[:, cols] = wout[cols, :].T

    for k in range(1, nb):
        came = image_rows(k, core)
        image_z(k, came).wait_recv()
        send(image_f(k, came))
    for k in range(1, nb):
        image_f(k, image_rows(k, 1 - core)).wait_recv()
    raw = img[...].astype(jnp.float32)
    imgu[...] = (raw * lax.rsqrt(jnp.sum(raw * raw, axis=1, keepdims=True) + EPSILON)).astype(jnp.bfloat16)

    score_shape = (piece, nb * per)
    label_col = lax.broadcasted_iota(jnp.int32, score_shape, 1)
    label_row = lax.broadcasted_iota(jnp.int32, score_shape, 0)
    wanted = jnp.zeros(score_shape, jnp.int32)
    for i in range(piece):
        wanted = jnp.where(label_row == i, pairs[b * piece + i], wanted)
    labels = (label_col == wanted).astype(jnp.float32)

    embedding = part[pl.ds(pl.multiple_of(b * piece, piece), piece), :]
    for k in range(1, nb):
        rs_copy(k).wait_recv()
        embedding = embedding + rs_recv[k].astype(jnp.float32)
    inv_norm = lax.rsqrt(jnp.sum(embedding * embedding, axis=1, keepdims=True) + EPSILON)
    unit = embedding * inv_norm
    logits = SCORE_SCALE * lax.dot_general(
        unit.astype(jnp.bfloat16), imgu[...], NT, preferred_element_type=jnp.float32
    ) + SCORE_BIAS_TERM
    mismatch = (1.0 / (1.0 + jnp.exp(-logits)) - labels).astype(jnp.bfloat16)
    unit_grad = SCORE_SCALE * jnp.dot(mismatch, imgu[...], preferred_element_type=jnp.float32)
    embed_grad = (unit_grad - unit * jnp.sum(unit * unit_grad, axis=1, keepdims=True)) * inv_norm
    mine = piece_rows(d, b)
    emb[mine, :] = embed_grad.astype(jnp.bfloat16)

    def ez_copy(kz, where):
        return remote(emb, where, ez_send.at[kz], ez_recv.at[kz], d, z_at(kz))

    def ex_copy(r, kz, dev):
        return remote(emb, piece_rows(dev, z_from(kz)), ex_send.at[r, kz], ex_recv.at[r, kz], peer(r))

    def ea_copy(k, z):
        return remote(emb, piece_rows(peer(3), z), ea_send.at[k], ea_recv.at[k], d, z_at(k))

    def ef_copy(r, kz, dev):
        return remote(emb, piece_rows(dev, z_from(kz)), ef_send.at[r, kz], ef_recv.at[r, kz], sibling)

    for kz in range(1, nb):
        send(ez_copy(kz, mine))

    def forward_on(r, kz):
        ex_copy(r, kz, peer(r)).wait_recv()
        send(ef_copy(r, kz, peer(r)))

    def forward_chip(r):
        if r:
            forward(chip_rows(chips[r]), far(r))
        caps_t[:, far(r)] = lax.dot_general(
            pick[...], caps[chip_rows(chips[r]), :], NT, preferred_element_type=jnp.float32
        ).astype(jnp.bfloat16)

    stores = []

    def store(src, dst):
        stores.append(pltpu.make_async_copy(src, dst, store_sem.at[len(stores)]))
        stores[-1].start()

    def backward_chip(r):
        for kz in range(nb):
            ef_copy(r, kz, other(r)).wait_recv()

        @pl.loop(0, ff // CHUNK)
        def _(j):
            cols = pl.ds(pl.multiple_of(j * CHUNK, CHUNK), CHUNK)
            back = jnp.dot(emb[chip_rows(chips[r]), :], wout_t[:, cols], preferred_element_type=jnp.float32)
            pgrad[far(r), cols] = (back * slope[far(r), cols]).astype(jnp.bfloat16)

        store(pgrad.at[far(r)], pgrad_hbm.at[far(r)])
        emb_t[:, far(r)] = lax.dot_general(
            pick[...], emb[chip_rows(chips[r]), :], NT, preferred_element_type=jnp.float32
        ).astype(jnp.bfloat16)

    for r in (3, 1, 2):
        send(ex_copy(r, 0, d))
    send(ef_copy(0, 0, d))

    for r in (1, 2, 3):
        remote(caps, dev_rows(peer(r)), cap_send.at[r], cap_recv.at[r], peer(r)).wait_recv()
        send(remote(caps, dev_rows(peer(r)), cap_fsend.at[r], cap_frecv.at[r], sibling))
    forward_chip(0)

    for kz in range(1, nb):
        ez_copy(kz, piece_rows(d, z_from(kz))).wait_recv()
        for r in (1, 2):
            send(ex_copy(r, kz, d))
        send(ef_copy(0, kz, d))
        if kz == 1:
            forward_on(3, 0)
            for k in range(1, nb):
                send(ea_copy(k, b))
    for r in (1, 2):
        forward_on(r, 0)

    def caption_wait(r):
        remote(caps, dev_rows(other(r)), cap_fsend.at[r], cap_frecv.at[r], sibling).wait_recv()

    caption_wait(1)
    forward_chip(1)
    for kz in range(1, nb):
        for r in (1, 2):
            forward_on(r, kz)
    caption_wait(2)
    forward_chip(2)
    for kz in range(1, nb):
        ea_copy(kz, z_from(kz)).wait_recv()
        send(ef_copy(3, kz, peer(3)))
    caption_wait(3)
    forward_chip(3)
    store(hidden, hidden_hbm)
    store(caps_t, capst_hbm)
    backward_chip(0)
    backward_chip(1)
    backward_chip(2)
    backward_chip(3)
    store(emb_t, embt_hbm)

    for copy in started:
        copy.wait_send()
    for copy in stores:
        copy.wait()


def product_kernel(caps_t, pgrad, emb_t, hidden, gin, gout):
    gin[...] = jnp.dot(caps_t[...], pgrad[...], preferred_element_type=jnp.float32)
    gout[...] = jnp.dot(emb_t[...], hidden[...], preferred_element_type=jnp.float32)


def fused_body(nd, nb, captions, w_in, w_out, images, pairs):
    rows, width = captions.shape
    ff = w_in.shape[1]
    per = images.shape[0]
    piece = rows // nb
    outs = width // nd
    half, single = jnp.bfloat16, jnp.float32
    dma = pltpu.SemaphoreType.DMA
    vmem = pltpu.VMEM
    anywhere = pl.BlockSpec(memory_space=pl.ANY)
    hidden, pgrad, caps_t, emb_t = pl.pallas_call(
        functools.partial(head_kernel, nd, nb),
        out_shape=[
            jax.ShapeDtypeStruct((nd * rows, ff), half),
            jax.ShapeDtypeStruct((nd * rows, ff), half),
            jax.ShapeDtypeStruct((outs, nd * rows), half),
            jax.ShapeDtypeStruct((outs, nd * rows), half),
        ],
        in_specs=[anywhere] * 4 + [pl.BlockSpec(memory_space=pltpu.SMEM)],
        out_specs=[anywhere] * 4,
        scratch_shapes=[
            vmem((width, ff), half),
            vmem((ff, width), half),
            vmem((width, ff), half),
            vmem((nb * per, width), half),
            vmem((nb * per, width), half),
            vmem((nd * rows, width), half),
            vmem((nd * rows, width), half),
            vmem((rows, width), single),
            vmem((rows, width), half),
            vmem((nb, piece, width), half),
            vmem((nd * rows, ff), half),
            vmem((nd * rows, ff), single),
            vmem((nd * rows, ff), half),
            vmem((outs, width), half),
            vmem((outs, nd * rows), half),
            vmem((outs, nd * rows), half),
            dma((4,)),
            dma((7,)),
            dma((4,)), dma((4,)), dma((4,)), dma((4,)),
            dma((nb,)), dma((nb,)), dma((nb,)), dma((nb,)),
            dma((nb,)), dma((nb,)),
            dma((nb,)), dma((nb,)), dma((nb,)), dma((nb,)),
            dma((4, nb)), dma((4, nb)), dma((4, nb)), dma((4, nb)),
        ],
        compiler_params=pltpu.CompilerParams(
            collective_id=0, has_side_effects=True, vmem_limit_bytes=VMEM_BYTES
        ),
    )(captions, w_in, w_out, images, pairs)
    left = pl.BlockSpec((outs, nd * rows), lambda j: (0, 0))
    right = pl.BlockSpec((nd * rows, WIDE), lambda j: (0, j))
    result = pl.BlockSpec((outs, WIDE), lambda j: (0, j))
    return pl.pallas_call(
        product_kernel,
        grid=(ff // WIDE,),
        out_shape=[jax.ShapeDtypeStruct((outs, ff), single)] * 2,
        in_specs=[left, right, left, right],
        out_specs=[result] * 2,
        compiler_params=pltpu.CompilerParams(vmem_limit_bytes=VMEM_BYTES),
    )(caps_t, pgrad, emb_t, hidden)


def fits(nd, nb, captions, w_in, images):
    rows, width = captions.shape
    ff = w_in.shape[1]
    per = images.shape[0]
    scratch = (
        6 * width * ff
        + 4 * nb * per * width
        + 4 * nd * rows * width
        + 16 * rows * width
        + 8 * nd * rows * ff
    )
    return (
        nd == 8
        and 1 < nb <= 4
        and ff % CHUNK == 0
        and ff % WIDE == 0
        and rows % (16 * nb) == 0
        and rows % 64 == 0
        and per % 32 == 0
        and width % (16 * nd) == 0
        and scratch < VMEM_BYTES * 3 // 4
    )


def body(captions, w_in, w_out, images, pairs):
    nd, nb = lax.axis_size("dp"), lax.axis_size("blk")
    if fits(nd, nb, captions, w_in, images):
        return tuple(fused_body(nd, nb, captions, w_in, w_out, images, pairs))
    return staged_body(captions, w_in, w_out, images, pairs)


def solution(mesh):
    return jax.shard_map(
        body,
        mesh=mesh,
        in_specs=(P("dp", None), P(None, "blk"), P("blk", None), P("blk", None), P("dp")),
        out_specs=(P("dp", "blk"), P("dp", "blk")),
        check_vma=False,
    )
```

```python
import functools

import jax
import jax.numpy as jnp
from jax import lax
from jax.experimental import pallas as pl
from jax.experimental.pallas import tpu as pltpu
from jax.sharding import PartitionSpec as P

SCORE_SCALE = 10.0
SCORE_BIAS_TERM = -5.0
EPSILON = 1e-06


def from_behind(block, axis, distance):
    devices = range(lax.axis_size(axis))
    route = [((i - distance) % len(devices), i) for i in devices]
    return lax.ppermute(block, axis, route)


def activate(values):
    return jax.nn.gelu(values, approximate=True)


def tile_grad(direction_halfway, image_direction, first_image, row_pairs):
    pair_scores = (
        SCORE_SCALE
        * lax.dot_general(
            direction_halfway,
            image_direction,
            (((1,), (1,)), ((), ())),
            preferred_element_type=jnp.float32,
        )
        + SCORE_BIAS_TERM
    )
    columns = first_image + lax.broadcasted_iota(jnp.int32, pair_scores.shape, 1)
    labels = (row_pairs[:, None] == columns).astype(jnp.float32)
    label_error = (jax.nn.sigmoid(pair_scores) - labels).astype(jnp.bfloat16)
    return SCORE_SCALE * jnp.dot(label_error, image_direction, preferred_element_type=jnp.float32)


def staged_body(captions, w_in, w_out, images, pairs):
    cycle_size = lax.axis_size("blk")
    cycle_pos = lax.axis_index("blk")
    own_rows = captions.shape[0] // cycle_size
    block_len = images.shape[0]
    width = captions.shape[1]
    pre_act = jnp.dot(captions, w_in, preferred_element_type=jnp.float32)
    hidden = activate(pre_act).astype(jnp.bfloat16)
    rows_hidden = hidden
    embedding = lax.psum_scatter(
        jnp.dot(rows_hidden, w_out, preferred_element_type=jnp.float32),
        "blk",
        scatter_dimension=0,
        tiled=True,
    )
    inv_norm = lax.rsqrt(jnp.sum(embedding * embedding, axis=1, keepdims=True) + EPSILON)
    unit_dir = embedding * inv_norm
    direction_halfway = unit_dir.astype(jnp.bfloat16)
    image_vals = images.astype(jnp.float32)
    image_direction = (
        image_vals * lax.rsqrt(jnp.sum(image_vals * image_vals, axis=1, keepdims=True) + EPSILON)
    ).astype(jnp.bfloat16)
    row_pairs = lax.dynamic_slice_in_dim(pairs, cycle_pos * own_rows, own_rows, 0)

    def visit(step, carry):
        running, block = carry
        source = (cycle_pos - step) % cycle_size
        running = running + tile_grad(direction_halfway, block, source * block_len, row_pairs)
        block = from_behind(block, "blk", 1)
        return (running, block)

    start_sum = jnp.zeros((own_rows, width), jnp.float32)
    running, block = lax.fori_loop(0, cycle_size - 1, visit, (start_sum, image_direction))
    source = (cycle_pos - (cycle_size - 1)) % cycle_size
    direction_gradient = running + tile_grad(
        direction_halfway, block, source * block_len, row_pairs
    )
    embed_grad = (
        direction_gradient
        - unit_dir * jnp.sum(unit_dir * direction_gradient, axis=1, keepdims=True)
    ) * inv_norm
    embed_half = embed_grad.astype(jnp.bfloat16)
    piece = lax.all_gather(embed_half, "blk", axis=0, tiled=True)
    rows_hidden = hidden
    hidden_grad = lax.dot_general(
        piece, w_out, (((1,), (1,)), ((), ())), preferred_element_type=jnp.float32
    )
    _, pullback = jax.vjp(activate, pre_act)
    preact_grad = pullback(hidden_grad)[0].astype(jnp.bfloat16)
    grad_in = lax.dot_general(
        captions, preact_grad, (((0,), (0,)), ((), ())), preferred_element_type=jnp.float32
    )
    grad_out = lax.dot_general(
        piece, rows_hidden, (((0,), (0,)), ((), ())), preferred_element_type=jnp.float32
    )
    grad_in, grad_out = (grad_in, grad_out)
    grad_w_in, grad_w_out_t = (
        lax.psum_scatter(grad_in, "dp", scatter_dimension=0, tiled=True),
        lax.psum_scatter(grad_out, "dp", scatter_dimension=0, tiled=True),
    )
    return (grad_w_in, grad_w_out_t)


MESH = pl.DeviceIdType.MESH
CHUNK = 256
WIDE = 512
VMEM_BYTES = 60 * 2**20
GELU_SCALE = 0.7978845608028654
GELU_CUBE = 0.044715
NT = (((1,), (1,)), ((), ()))


def gelu_and_slope(v):
    square = v * v
    t = jnp.tanh(GELU_SCALE * (v + GELU_CUBE * (square * v)))
    half = 0.5 * (1.0 + t)
    slope = half + (0.5 * GELU_SCALE) * v * (1.0 - t * t) * (1.0 + (3.0 * GELU_CUBE) * square)
    return v * half, slope


def head_kernel(
    nd, nb,
    caps_hbm, win_hbm, wout_hbm, img_hbm, pairs, hidden_hbm, pgrad_hbm, capst_hbm, embt_hbm,
    win, wout, wout_t, img, imgu, caps, emb, part, rs_send, rs_recv, hidden, slope, pgrad,
    pick, caps_t, emb_t,
    load_sem, store_sem,
    cap_send, cap_recv, cap_fsend, cap_frecv,
    img_send, img_recv, img_fsend, img_frecv,
    rs_ssem, rs_rsem,
    ez_send, ez_recv, ea_send, ea_recv, ex_send, ex_recv, ef_send, ef_recv,
):
    d = lax.axis_index("dp")
    b = lax.axis_index("blk")
    core = d % 2
    chip = d // 2
    chips = (chip, chip + 1 - 2 * (chip % 2), (chip + 2) % 4, 3 - chip)
    sibling = chip * 2 + (1 - core)
    rows, width = caps_hbm.shape
    ff = win_hbm.shape[1]
    per = img_hbm.shape[0]
    half = per // 2
    piece = rows // nb

    def z_at(k):
        return (b + k) % nb

    def z_from(k):
        return (b + nb - k) % nb

    def peer(r):
        return chips[r] * 2 + core

    def other(r):
        return chips[r] * 2 + (1 - core)

    def dev_rows(dev, part=0, parts=1):
        size = rows // parts
        return pl.ds(pl.multiple_of(dev * rows + part * size, size), size)

    def chip_rows(c):
        return pl.ds(pl.multiple_of(c * (2 * rows), 2 * rows), 2 * rows)

    def piece_rows(dev, z):
        return pl.ds(pl.multiple_of(dev * rows + z * piece, piece), piece)

    def image_rows(k, side):
        return pl.ds(pl.multiple_of(z_from(k) * per + side * half, half), half)

    def remote(ref, where, send, recv, dp, blk=b):
        return pltpu.make_async_remote_copy(
            src_ref=ref.at[where], dst_ref=ref.at[where], send_sem=send, recv_sem=recv,
            device_id=(dp, blk), device_id_type=MESH,
        )

    started = []

    def send(copy):
        copy.start()
        started.append(copy)

    own = dev_rows(d)
    own_images = pl.ds(pl.multiple_of(b * per, per), per)
    loads = [
        pltpu.make_async_copy(caps_hbm, caps.at[own], load_sem.at[0]),
        pltpu.make_async_copy(win_hbm, win, load_sem.at[1]),
        pltpu.make_async_copy(wout_hbm, wout, load_sem.at[2]),
        pltpu.make_async_copy(img_hbm, img.at[own_images], load_sem.at[3]),
    ]
    for load in loads:
        load.start()

    barrier = pltpu.get_barrier_semaphore()
    for k in range(1, nb):
        pl.semaphore_signal(barrier, inc=1, device_id=(d, z_at(k)), device_id_type=MESH)
    for r in (1, 2, 3):
        pl.semaphore_signal(barrier, inc=1, device_id=(peer(r), b), device_id_type=MESH)
    pl.semaphore_signal(barrier, inc=1, device_id=(sibling, b), device_id_type=MESH)

    def forward(source, target):
        @pl.loop(0, ff // CHUNK)
        def _(j):
            cols = pl.ds(pl.multiple_of(j * CHUNK, CHUNK), CHUNK)
            pre = jnp.dot(caps[source, :], win[:, cols], preferred_element_type=jnp.float32)
            h, s = gelu_and_slope(pre)
            hidden[target, cols] = h.astype(jnp.bfloat16)
            slope[target, cols] = s

    def near(side):
        return pl.ds(pl.multiple_of(side * rows, rows), rows)

    def far(r):
        return pl.ds(r * 2 * rows, 2 * rows)

    loads[0].wait()
    loads[1].wait()
    forward(own, near(core))
    loads[2].wait()
    part[...] = jnp.dot(hidden[near(core), :], wout[...], preferred_element_type=jnp.float32)
    rs_send[...] = part[...].astype(jnp.bfloat16)
    loads[3].wait()

    pl.semaphore_wait(barrier, nb + 3)

    def rs_copy(k):
        away = pl.ds(pl.multiple_of(z_at(k) * piece, piece), piece)
        return pltpu.make_async_remote_copy(
            src_ref=rs_send.at[away], dst_ref=rs_recv.at[k], send_sem=rs_ssem.at[k],
            recv_sem=rs_rsem.at[k], device_id=(d, z_at(k)), device_id_type=MESH,
        )

    def image_z(k, where):
        return remote(img, where, img_send.at[k], img_recv.at[k], d, z_at(k))

    def image_f(k, where):
        return remote(img, where, img_fsend.at[k], img_frecv.at[k], sibling)

    for k in range(1, nb):
        send(rs_copy(k))
    for k in range(1, nb):
        send(image_z(k, image_rows(0, core)))
    send(remote(caps, own, cap_fsend.at[0], cap_frecv.at[0], sibling))
    for r in (1, 2, 3):
        send(remote(caps, own, cap_send.at[r], cap_recv.at[r], peer(r)))

    columns = lax.broadcasted_iota(jnp.int32, pick.shape, 1)
    lines = lax.broadcasted_iota(jnp.int32, pick.shape, 0)
    pick[...] = (columns == lines + d * pick.shape[0]).astype(jnp.float32).astype(jnp.bfloat16)

    remote(caps, dev_rows(sibling), cap_fsend.at[0], cap_frecv.at[0], sibling).wait_recv()
    forward(dev_rows(sibling), near(1 - core))

    @pl.loop(0, ff // CHUNK)
    def _(j):
        cols = pl.ds(pl.multiple_of(j * CHUNK, CHUNK), CHUNK)
        wout_t[:, cols] = wout[cols, :].T

    for k in range(1, nb):
        came = image_rows(k, core)
        image_z(k, came).wait_recv()
        send(image_f(k, came))
    for k in range(1, nb):
        image_f(k, image_rows(k, 1 - core)).wait_recv()
    raw = img[...].astype(jnp.float32)
    imgu[...] = (raw * lax.rsqrt(jnp.sum(raw * raw, axis=1, keepdims=True) + EPSILON)).astype(jnp.bfloat16)

    score_shape = (piece, nb * per)
    label_col = lax.broadcasted_iota(jnp.int32, score_shape, 1)
    label_row = lax.broadcasted_iota(jnp.int32, score_shape, 0)
    wanted = jnp.zeros(score_shape, jnp.int32)
    for i in range(piece):
        wanted = jnp.where(label_row == i, pairs[b * piece + i], wanted)
    labels = (label_col == wanted).astype(jnp.float32)

    embedding = part[pl.ds(pl.multiple_of(b * piece, piece), piece), :]
    for k in range(1, nb):
        rs_copy(k).wait_recv()
        embedding = embedding + rs_recv[k].astype(jnp.float32)
    inv_norm = lax.rsqrt(jnp.sum(embedding * embedding, axis=1, keepdims=True) + EPSILON)
    unit = embedding * inv_norm
    logits = SCORE_SCALE * lax.dot_general(
        unit.astype(jnp.bfloat16), imgu[...], NT, preferred_element_type=jnp.float32
    ) + SCORE_BIAS_TERM
    mismatch = (1.0 / (1.0 + jnp.exp(-logits)) - labels).astype(jnp.bfloat16)
    unit_grad = SCORE_SCALE * jnp.dot(mismatch, imgu[...], preferred_element_type=jnp.float32)
    embed_grad = (unit_grad - unit * jnp.sum(unit * unit_grad, axis=1, keepdims=True)) * inv_norm
    mine = piece_rows(d, b)
    emb[mine, :] = embed_grad.astype(jnp.bfloat16)

    def ez_copy(kz, where):
        return remote(emb, where, ez_send.at[kz], ez_recv.at[kz], d, z_at(kz))

    def ex_copy(r, kz, dev):
        return remote(emb, piece_rows(dev, z_from(kz)), ex_send.at[r, kz], ex_recv.at[r, kz], peer(r))

    def ea_copy(k, z):
        return remote(emb, piece_rows(peer(3), z), ea_send.at[k], ea_recv.at[k], d, z_at(k))

    def ef_copy(r, kz, dev):
        return remote(emb, piece_rows(dev, z_from(kz)), ef_send.at[r, kz], ef_recv.at[r, kz], sibling)

    for kz in range(1, nb):
        send(ez_copy(kz, mine))

    def forward_on(r, kz):
        ex_copy(r, kz, peer(r)).wait_recv()
        send(ef_copy(r, kz, peer(r)))

    def forward_chip(r):
        if r:
            forward(chip_rows(chips[r]), far(r))
        caps_t[:, far(r)] = lax.dot_general(
            pick[...], caps[chip_rows(chips[r]), :], NT, preferred_element_type=jnp.float32
        ).astype(jnp.bfloat16)

    stores = []

    def store(src, dst):
        stores.append(pltpu.make_async_copy(src, dst, store_sem.at[len(stores)]))
        stores[-1].start()

    def backward_chip(r):
        for kz in range(nb):
            ef_copy(r, kz, other(r)).wait_recv()

        @pl.loop(0, ff // CHUNK)
        def _(j):
            cols = pl.ds(pl.multiple_of(j * CHUNK, CHUNK), CHUNK)
            back = jnp.dot(emb[chip_rows(chips[r]), :], wout_t[:, cols], preferred_element_type=jnp.float32)
            pgrad[far(r), cols] = (back * slope[far(r), cols]).astype(jnp.bfloat16)

        store(pgrad.at[far(r)], pgrad_hbm.at[far(r)])
        emb_t[:, far(r)] = lax.dot_general(
            pick[...], emb[chip_rows(chips[r]), :], NT, preferred_element_type=jnp.float32
        ).astype(jnp.bfloat16)

    for r in (3, 1, 2):
        send(ex_copy(r, 0, d))
    send(ef_copy(0, 0, d))

    for r in (1, 2, 3):
        remote(caps, dev_rows(peer(r)), cap_send.at[r], cap_recv.at[r], peer(r)).wait_recv()
        send(remote(caps, dev_rows(peer(r)), cap_fsend.at[r], cap_frecv.at[r], sibling))
    forward_chip(0)

    for kz in range(1, nb):
        ez_copy(kz, piece_rows(d, z_from(kz))).wait_recv()
        for r in (1, 2):
            send(ex_copy(r, kz, d))
        send(ef_copy(0, kz, d))
        if kz == 1:
            forward_on(3, 0)
            for k in range(1, nb):
                send(ea_copy(k, b))
    for r in (1, 2):
        forward_on(r, 0)

    def caption_wait(r):
        remote(caps, dev_rows(other(r)), cap_fsend.at[r], cap_frecv.at[r], sibling).wait_recv()

    for r in (1, 2):
        caption_wait(r)
        forward_chip(r)
    backward_chip(0)
    for kz in range(1, nb):
        for r in (1, 2):
            forward_on(r, kz)
    caption_wait(3)
    forward_chip(3)
    store(hidden, hidden_hbm)
    store(caps_t, capst_hbm)
    backward_chip(1)
    for kz in range(1, nb):
        ea_copy(kz, z_from(kz)).wait_recv()
        send(ef_copy(3, kz, peer(3)))
    backward_chip(2)
    backward_chip(3)
    store(emb_t, embt_hbm)

    for copy in started:
        copy.wait_send()
    for copy in stores:
        copy.wait()


def product_kernel(caps_t, pgrad, emb_t, hidden, gin, gout):
    gin[...] = jnp.dot(caps_t[...], pgrad[...], preferred_element_type=jnp.float32)
    gout[...] = jnp.dot(emb_t[...], hidden[...], preferred_element_type=jnp.float32)


def fused_body(nd, nb, captions, w_in, w_out, images, pairs):
    rows, width = captions.shape
    ff = w_in.shape[1]
    per = images.shape[0]
    piece = rows // nb
    outs = width // nd
    half, single = jnp.bfloat16, jnp.float32
    dma = pltpu.SemaphoreType.DMA
    vmem = pltpu.VMEM
    anywhere = pl.BlockSpec(memory_space=pl.ANY)
    hidden, pgrad, caps_t, emb_t = pl.pallas_call(
        functools.partial(head_kernel, nd, nb),
        out_shape=[
            jax.ShapeDtypeStruct((nd * rows, ff), half),
            jax.ShapeDtypeStruct((nd * rows, ff), half),
            jax.ShapeDtypeStruct((outs, nd * rows), half),
            jax.ShapeDtypeStruct((outs, nd * rows), half),
        ],
        in_specs=[anywhere] * 4 + [pl.BlockSpec(memory_space=pltpu.SMEM)],
        out_specs=[anywhere] * 4,
        scratch_shapes=[
            vmem((width, ff), half),
            vmem((ff, width), half),
            vmem((width, ff), half),
            vmem((nb * per, width), half),
            vmem((nb * per, width), half),
            vmem((nd * rows, width), half),
            vmem((nd * rows, width), half),
            vmem((rows, width), single),
            vmem((rows, width), half),
            vmem((nb, piece, width), half),
            vmem((nd * rows, ff), half),
            vmem((nd * rows, ff), single),
            vmem((nd * rows, ff), half),
            vmem((outs, width), half),
            vmem((outs, nd * rows), half),
            vmem((outs, nd * rows), half),
            dma((4,)),
            dma((7,)),
            dma((4,)), dma((4,)), dma((4,)), dma((4,)),
            dma((nb,)), dma((nb,)), dma((nb,)), dma((nb,)),
            dma((nb,)), dma((nb,)),
            dma((nb,)), dma((nb,)), dma((nb,)), dma((nb,)),
            dma((4, nb)), dma((4, nb)), dma((4, nb)), dma((4, nb)),
        ],
        compiler_params=pltpu.CompilerParams(
            collective_id=0, has_side_effects=True, vmem_limit_bytes=VMEM_BYTES
        ),
    )(captions, w_in, w_out, images, pairs)
    left = pl.BlockSpec((outs, nd * rows), lambda j: (0, 0))
    right = pl.BlockSpec((nd * rows, WIDE), lambda j: (0, j))
    result = pl.BlockSpec((outs, WIDE), lambda j: (0, j))
    return pl.pallas_call(
        product_kernel,
        grid=(ff // WIDE,),
        out_shape=[jax.ShapeDtypeStruct((outs, ff), single)] * 2,
        in_specs=[left, right, left, right],
        out_specs=[result] * 2,
        compiler_params=pltpu.CompilerParams(vmem_limit_bytes=VMEM_BYTES),
    )(caps_t, pgrad, emb_t, hidden)


def fits(nd, nb, captions, w_in, images):
    rows, width = captions.shape
    ff = w_in.shape[1]
    per = images.shape[0]
    scratch = (
        6 * width * ff
        + 4 * nb * per * width
        + 4 * nd * rows * width
        + 16 * rows * width
        + 8 * nd * rows * ff
    )
    return (
        nd == 8
        and 1 < nb <= 4
        and ff % CHUNK == 0
        and ff % WIDE == 0
        and rows % (16 * nb) == 0
        and rows % 64 == 0
        and per % 32 == 0
        and width % (16 * nd) == 0
        and scratch < VMEM_BYTES * 3 // 4
    )


def body(captions, w_in, w_out, images, pairs):
    nd, nb = lax.axis_size("dp"), lax.axis_size("blk")
    if fits(nd, nb, captions, w_in, images):
        return tuple(fused_body(nd, nb, captions, w_in, w_out, images, pairs))
    return staged_body(captions, w_in, w_out, images, pairs)


def solution(mesh):
    return jax.shard_map(
        body,
        mesh=mesh,
        in_specs=(P("dp", None), P(None, "blk"), P("blk", None), P("blk", None), P("dp")),
        out_specs=(P("dp", "blk"), P("dp", "blk")),
        check_vma=False,
    )
```
